512 devices in a mesh: seq: 8 (over y, core), fsdp: 16 (over z), dp: 4 (over x).
Axes of the slice: x: 4, y: 4, z: 16, core: 2. Of those that a mesh axis runs over, the one named last changes fastest.
Arguments:
- query_in: bfloat16 [64, 1024, 1536], P(('fsdp', 'dp'), 'seq'), may hold values from -8 to 8
- key_in: bfloat16 [64, 1024, 1536], P(('fsdp', 'dp'), 'seq'), may hold values from -8 to 8
- value_in: bfloat16 [64, 1024, 1536], P(('fsdp', 'dp'), 'seq'), may hold values from -24 to 24
- out_grad: bfloat16 [64, 1024, 1536], P(('fsdp', 'dp'), 'seq'), may hold values from -16 to 16
- out_weight: bfloat16 [1536, 1536], P('seq', 'fsdp'), may hold values from -0.15625 to 0.15625
- key_tiles: int32 [64, 24, 32, 6], P(('fsdp', 'dp'), 'seq'), may hold values from 0 to 31, as said below
- key_count: int32 [64, 24, 32], P(('fsdp', 'dp'), 'seq'), may hold values from 1 to 6, as said below
Outputs:
- layer_out: bfloat16 [64, 1024, 1536], P(('fsdp', 'dp'), 'seq')
- query_grad: bfloat16 [64, 1024, 1536], P(('fsdp', 'dp'), 'seq')
- key_grad: bfloat16 [64, 1024, 1536], P(('fsdp', 'dp'), 'seq')
- value_grad: bfloat16 [64, 1024, 1536], P(('fsdp', 'dp'), 'seq')
- weight_grad: float32 [1536, 1536], P('seq', ('fsdp', 'dp'))
The draws below stay inside these ranges and needn't reach their ends.
Inputs may be any that keep to these rules, and one draw needn't show every extreme that they name: Tile m lies in frame m // 2, row (m) % 2 and column m % 1 of a grid of 16 frames. The first key_count[c, h, n] entries of key_tiles[c, h, n, :] are, in some order, the distinct tiles whose frame, row and column differ from those of tile n by at most the frame, row and column reach of head h in clip c, each 0 or 1; the remaining entries are arbitrary tile numbers. `key_count`: the number of live entries of each list; every clip has a list with 6.
All inputs are finite; a program needn't handle non-finite values.
Results may differ from the reference program's by a relative error of at most 0.02.
Values may be sent and summed in bfloat16 or wider, within the bound.
No kernel may reach another device: no remote copies, remote signals or barrier semaphores. Data moves between devices by JAX's collectives and lax.ppermute only.
A program may use at most 128 MiB of HBM per device.

```python
import jax
import jax.numpy as jnp
from jax import lax

D = 1536
HEADS = 24
HD = 64
TILE = 32
GR = 2
GC = 1
S = 1024
NT = 32
GF = 16
KSLOT = 6
CLIPS = 64


def drawn_pair(key):
    full_shape = (CLIPS, S, HEADS * HD)
    query_base = jax.random.truncated_normal(jax.random.fold_in(key, 11), -6.0, 6.0, full_shape, jnp.float32)
    key_base = jax.random.truncated_normal(jax.random.fold_in(key, 12), -6.0, 6.0, full_shape, jnp.float32)
    return (query_base, key_base)


def draw_query_in(key, part):
    return drawn_pair(key)[0].astype(jnp.bfloat16)


def draw_key_in(key, part):
    return drawn_pair(key)[1].astype(jnp.bfloat16)


def tile_windows(key):
    radius = jax.random.randint(jax.random.fold_in(key, 21), (CLIPS, HEADS, 3), 0, 2)
    chosen = jax.random.randint(jax.random.fold_in(key, 22), (CLIPS, 1), 0, HEADS)
    forced = (jnp.arange(HEADS)[None, :] == chosen)[:, :, None]
    radius = jnp.where(forced, 1, radius)
    tile_ids = jnp.arange(NT)
    tile_frame = tile_ids // (GR * GC)
    tile_row = tile_ids // GC % GR
    tile_col = tile_ids % GC
    offsets = jnp.arange(27)
    step_frame = offsets // 9 - 1
    step_row = offsets // 3 % 3 - 1
    step_col = offsets % 3 - 1
    near_frame = tile_frame[:, None] + step_frame[None, :]
    near_row = tile_row[:, None] + step_row[None, :]
    near_col = tile_col[:, None] + step_col[None, :]
    inside = (near_frame >= 0) & (near_frame < GF) & (near_row >= 0) & (near_row < GR) & (near_col >= 0) & (near_col < GC)
    reach = (jnp.abs(step_frame)[None, None, None, :] <= radius[:, :, None, 0:1]) & (jnp.abs(step_row)[None, None, None, :] <= radius[:, :, None, 1:2]) & (jnp.abs(step_col)[None, None, None, :] <= radius[:, :, None, 2:3])
    live = inside[None, None, :, :] & reach
    target = jnp.clip(near_frame, 0, GF - 1) * (GR * GC) + jnp.clip(near_row, 0, GR - 1) * GC + jnp.clip(near_col, 0, GC - 1)
    target = jnp.broadcast_to(target[None, None, :, :], live.shape)
    scores = jax.random.randint(jax.random.fold_in(key, 23), live.shape, 0, 1000) * 32 + offsets[None, None, None, :]
    ranking = jnp.argsort(jnp.where(live, scores, scores + 100000), axis=-1, stable=True)
    ranked = jnp.take_along_axis(target, ranking, axis=-1)[..., :KSLOT]
    ranked_live = jnp.take_along_axis(live, ranking, axis=-1)[..., :KSLOT]
    filler = jax.random.randint(jax.random.fold_in(key, 24), ranked.shape, 0, NT)
    tile_lists = jnp.where(ranked_live, ranked, filler).astype(jnp.int32)
    counts = jnp.sum(live.astype(jnp.int32), axis=-1).astype(jnp.int32)
    return (tile_lists, counts)


def draw_key_tiles(key, part):
    return tile_windows(key)[0]


def draw_key_count(key, part):
    return tile_windows(key)[1]


def spiked(values, rng, source, target, shards_of, factor):
    def block_of(axis_at):
        return (jnp.arange(values.shape[axis_at]) // (values.shape[axis_at] // shards_of)).reshape((-1,) + (1,) * (values.ndim - 1 - axis_at))

    one_side = jax.random.permutation(rng, shards_of)[block_of(target)]
    other_side = (block_of(target) + shards_of // 2) % shards_of
    return jnp.where((block_of(source) == one_side) | (block_of(source) == other_side), factor * values, values)


def block_scale(rng, extent, pieces, low, top_value):
    level = 1.0
    for axis_at, shards_of in pieces:
        draws = jax.random.uniform(jax.random.fold_in(jax.random.fold_in(rng, 6), axis_at), (shards_of,), jnp.float32, low / len(pieces), top_value / len(pieces))
        level = level * jnp.repeat(jnp.exp(draws), extent[axis_at] // shards_of).reshape((-1,) + (1,) * (len(extent) - 1 - axis_at))
    return level


def gaussian(own_key, extent, scale, bound, pieces=(), held_as=jnp.bfloat16):
    drawn = scale * jax.random.normal(own_key, extent, jnp.float32)
    if pieces:
        drawn = drawn * block_scale(own_key, extent, pieces, -0.22, 0.18)
    return jnp.clip(drawn, -bound, bound).astype(held_as)


def bell_draw_with(stream_key, dims, scale, limit, shards, heavy, dtype=jnp.bfloat16):
    entries = scale * jax.random.normal(stream_key, dims, jnp.float32)
    if shards:
        entries = entries * block_scale(stream_key, dims, shards, -0.22, 0.18)
    return jnp.clip(spiked(entries, jax.random.fold_in(stream_key, 3), *heavy), -limit, limit).astype(dtype)


def setup_inputs(seed: int = 0) -> dict:
    splits = jax.random.split(jax.random.key(seed), 8)
    return {
        "query_in": draw_query_in(jax.random.fold_in(splits[7], 71), 0),
        "key_in": draw_key_in(jax.random.fold_in(splits[7], 71), 0),
        "value_in": gaussian(splits[2], (CLIPS, S, HEADS * HD), 4.0, 24.0, ((0, 64), (1, 8))),
        "out_grad": bell_draw_with(splits[3], (CLIPS, S, D), 1.0, 16.0, ((0, 64), (1, 8)), (0, 2, 64, 4.0)),
        "out_weight": gaussian(splits[4], (HEADS * HD, D), (HEADS * HD) ** -0.5, 0.15625, ((0, 8), (1, 16))),
        "key_tiles": draw_key_tiles(jax.random.fold_in(splits[7], 71), 0),
        "key_count": draw_key_count(jax.random.fold_in(splits[7], 71), 0),
    }


def head_forward(query_head, key_head, value_head, head_list, tile_counts):
    tile_number, tile_len, head_dim = query_head.shape
    slot_number = head_list.shape[1]
    score_scale = head_dim ** -0.5
    key_chosen = key_head[head_list].reshape(tile_number, slot_number * tile_len, head_dim).astype(jnp.float32)
    value_chosen = value_head[head_list].reshape(tile_number, slot_number * tile_len, head_dim).astype(jnp.float32)
    kept_mask = (jnp.arange(slot_number * tile_len) // tile_len)[None, :] < tile_counts[:, None]
    scores = jnp.einsum("nqd,nkd->nqk", query_head.astype(jnp.float32), key_chosen, precision=lax.Precision.HIGHEST) * score_scale
    scores = jnp.where(kept_mask[:, None, :], scores, -jnp.inf)
    row_max = jnp.max(scores, axis=-1, keepdims=True)
    log_total = row_max + jnp.log(jnp.sum(jnp.exp(scores - row_max), axis=-1, keepdims=True))
    rounded = jnp.exp(scores - log_total).astype(jnp.bfloat16)
    attended = jnp.einsum("nqk,nkd->nqd", rounded.astype(jnp.float32), value_chosen, precision=lax.Precision.HIGHEST).astype(jnp.bfloat16)
    return attended, log_total


def head_backward(query_head, key_head, value_head, head_list, tile_counts, attended, log_total, upstream):
    tile_number, tile_len, head_dim = query_head.shape
    slot_number = head_list.shape[1]
    score_scale = head_dim ** -0.5
    key_chosen = key_head[head_list].reshape(tile_number, slot_number * tile_len, head_dim).astype(jnp.float32)
    value_chosen = value_head[head_list].reshape(tile_number, slot_number * tile_len, head_dim).astype(jnp.float32)
    kept_mask = (jnp.arange(slot_number * tile_len) // tile_len)[None, :] < tile_counts[:, None]
    query_wide = query_head.astype(jnp.float32)
    upstream_wide = upstream.astype(jnp.float32)
    scores = jnp.einsum("nqd,nkd->nqk", query_wide, key_chosen, precision=lax.Precision.HIGHEST) * score_scale
    scores = jnp.where(kept_mask[:, None, :], scores, -jnp.inf)
    weights = jnp.exp(scores - log_total)
    rounded = weights.astype(jnp.bfloat16)
    inner_sum = jnp.sum(upstream_wide * attended.astype(jnp.float32), axis=-1, keepdims=True)
    prob_grad = jnp.einsum("nqd,nkd->nqk", upstream_wide, value_chosen, precision=lax.Precision.HIGHEST)
    score_grad = (weights * (prob_grad - inner_sum)).astype(jnp.bfloat16).astype(jnp.float32)
    query_grad = (jnp.einsum("nqk,nkd->nqd", score_grad, key_chosen, precision=lax.Precision.HIGHEST) * score_scale).astype(jnp.bfloat16)
    key_slots = jnp.einsum("nqk,nqd->nkd", score_grad, query_wide, precision=lax.Precision.HIGHEST) * score_scale
    value_slots = jnp.einsum("nqk,nqd->nkd", rounded.astype(jnp.float32), upstream_wide, precision=lax.Precision.HIGHEST)
    live_slots = jnp.arange(slot_number)[None, :] < tile_counts[:, None]
    one_hot = ((head_list[:, :, None] == jnp.arange(tile_number)[None, None, :]) & live_slots[:, :, None]).astype(jnp.float32)
    slot_shape = (tile_number, slot_number, tile_len, head_dim)
    key_grad = jnp.einsum("nst,nsrd->trd", one_hot, key_slots.reshape(slot_shape), precision=lax.Precision.HIGHEST).astype(jnp.bfloat16)
    value_grad = jnp.einsum("nst,nsrd->trd", one_hot, value_slots.reshape(slot_shape), precision=lax.Precision.HIGHEST).astype(jnp.bfloat16)
    return query_grad, key_grad, value_grad


def heads_to_rows(stacked):
    return jnp.transpose(stacked, (1, 2, 0, 3)).reshape(stacked.shape[1] * stacked.shape[2], stacked.shape[0] * stacked.shape[3])


def reference(query_in, key_in, value_in, out_grad, out_weight, key_tiles, key_count):
    grid_shape = (NT, TILE, HEADS, HD)

    def per_clip(weight_sum, clip_index):
        query_grid = query_in[clip_index].reshape(grid_shape)
        key_grid = key_in[clip_index].reshape(grid_shape)
        value_grid = value_in[clip_index].reshape(grid_shape)
        clip_lists = key_tiles[clip_index]
        clip_counts = key_count[clip_index]
        grad_rows = out_grad[clip_index]

        def pick_head(field, head_index):
            return lax.dynamic_index_in_dim(field, head_index, 2, keepdims=False)

        def forward_head(head_index):
            return head_forward(pick_head(query_grid, head_index), pick_head(key_grid, head_index), pick_head(value_grid, head_index), clip_lists[head_index], clip_counts[head_index])

        attended, log_total = lax.map(forward_head, jnp.arange(HEADS))
        attn_rows = heads_to_rows(attended)
        layer_out = jnp.dot(attn_rows, out_weight, preferred_element_type=jnp.float32).astype(jnp.bfloat16)
        upstream = jnp.dot(grad_rows, out_weight.T, preferred_element_type=jnp.float32).astype(jnp.bfloat16)
        upstream_grid = upstream.reshape(grid_shape)

        def backward_head(head_index):
            return head_backward(pick_head(query_grid, head_index), pick_head(key_grid, head_index), pick_head(value_grid, head_index), clip_lists[head_index], clip_counts[head_index], attended[head_index], log_total[head_index], pick_head(upstream_grid, head_index))

        query_back, key_back, value_back = lax.map(backward_head, jnp.arange(HEADS))
        weight_sum = weight_sum + jnp.dot(attn_rows.T, grad_rows, preferred_element_type=jnp.float32)
        return weight_sum, (layer_out, heads_to_rows(query_back), heads_to_rows(key_back), heads_to_rows(value_back))

    summed, stacked = lax.scan(per_clip, jnp.zeros((HEADS * HD, D), jnp.float32), jnp.arange(CLIPS))
    return stacked[0], stacked[1], stacked[2], stacked[3], summed / CLIPS
```

```python
import functools

import jax
import jax.numpy as jnp
from jax import lax
from jax.experimental import pallas as pl
from jax.experimental.pallas import tpu as pltpu
from jax.sharding import Mesh
from jax.sharding import PartitionSpec as P

BF16 = jnp.bfloat16
F32 = jnp.float32
HEAD_DIM = 64
FRAME = 64
SCORE_SCALE = HEAD_DIM ** (-0.5)
LOG2_E = 1.4426950408889634
DROPPED = -1e30
NT = (((1,), (1,)), ((), ()))
NN = (((1,), (0,)), ((), ()))


def dot(left, right, dims):
    return lax.dot_general(left, right, dims, preferred_element_type=F32)


def call(kernel, out_shape, operands, in_specs=None, scratch=()):
    vmem = pl.BlockSpec(memory_space=pltpu.VMEM)
    return pl.pallas_call(
        kernel,
        out_shape=out_shape,
        in_specs=in_specs or [vmem] * len(operands),
        out_specs=jax.tree.map(lambda _: vmem, out_shape),
        scratch_shapes=list(scratch),
        compiler_params=pltpu.CompilerParams(vmem_limit_bytes=56 * 2**20),
    )(*operands)


def pack_kernel(query_ref, key_ref, value_ref, out_ref):
    peers = out_ref.shape[0]
    width = query_ref.shape[1] // peers
    for place, ref in enumerate((query_ref, key_ref, value_ref)):
        turned = ref[...].T
        for peer in range(peers):
            out_ref[peer, place * width : (place + 1) * width, :] = turned[
                peer * width : (peer + 1) * width
            ]


def unpack_kernel(x_ref, *out_refs):
    peers = x_ref.shape[0]
    width = x_ref.shape[1] // len(out_refs)
    for place, ref in enumerate(out_refs):
        stacked = jnp.concatenate(
            [x_ref[peer, place * width : (place + 1) * width, :] for peer in range(peers)], axis=0
        )
        ref[...] = stacked.T


def join_columns_kernel(x_ref, out_ref):
    width = x_ref.shape[2]
    for place in range(x_ref.shape[0]):
        out_ref[:, place * width : (place + 1) * width] = x_ref[place]


def window_start(block, blocks, block_frames, window_frames):
    return min(max(block * block_frames - 1, 0), blocks * block_frames - window_frames)


def keep_bias(shift, keys, queries, count):
    key_at = lax.broadcasted_iota(jnp.int32, (keys, queries), 0)
    query_at = lax.broadcasted_iota(jnp.int32, (keys, queries), 1)
    frames_off = jnp.abs(key_at // FRAME + shift - query_at // FRAME)
    same_row = (key_at // 32) % 2 == (query_at // 32) % 2
    frame_reach = jnp.where(count >= 3, 1, 0)
    row_reach = jnp.where(count % 2 == 0, 1, 0)
    rows_off = jnp.where(same_row, 0, 1)
    return jnp.where((frames_off <= frame_reach) & (rows_off <= row_reach), 0.0, DROPPED)


def plan(x_ref):
    blocks, _, block_tokens = x_ref.shape
    block_frames = block_tokens // FRAME
    return blocks, block_tokens, block_frames, block_frames + 2


def rows_of(x_ref, part, head, local_heads):
    at = (part * local_heads + head) * HEAD_DIM
    return jnp.concatenate(
        [x_ref[block, at : at + HEAD_DIM, :] for block in range(x_ref.shape[0])], axis=1
    )


def forward_kernel(count_ref, x_ref, attended_ref, log_ref):
    local_heads = count_ref.shape[0]
    blocks, block_tokens, block_frames, window_frames = plan(x_ref)
    window = window_frames * FRAME
    for head in range(local_heads):
        count = count_ref[head, 2]
        query_t = rows_of(x_ref, 0, head, local_heads)
        key_rows = rows_of(x_ref, 1, head, local_heads).T
        value_t = rows_of(x_ref, 2, head, local_heads)
        biases = {}
        for block in range(blocks):
            first = window_start(block, blocks, block_frames, window_frames)
            shift = first - block * block_frames
            if shift not in biases:
                biases[shift] = keep_bias(shift, window, block_tokens, count)
            here = slice(block * block_tokens, (block + 1) * block_tokens)
            near = slice(first * FRAME, first * FRAME + window)
            scores = (
                dot(key_rows[near], query_t[:, here], NN) * (SCORE_SCALE * LOG2_E) + biases[shift]
            )
            top = jnp.max(scores, axis=0, keepdims=True)
            raw = jnp.exp2(scores - top)
            total = jnp.sum(raw, axis=0, keepdims=True)
            rounded = (raw * (1.0 / total)).astype(BF16)
            attended_ref[block, head * HEAD_DIM : (head + 1) * HEAD_DIM, :] = dot(
                value_t[:, near], rounded, NN
            ).astype(BF16)
            log_ref[head, :, here] = top + jnp.log2(total)


def backward_kernel(count_ref, x_ref, attended_ref, log_ref, up_ref, out_ref, key_sum, value_sum):
    local_heads = count_ref.shape[0]
    blocks, block_tokens, block_frames, window_frames = plan(x_ref)
    window = window_frames * FRAME
    for head in range(local_heads):
        count = count_ref[head, 2]
        query_t = rows_of(x_ref, 0, head, local_heads)
        key_t = rows_of(x_ref, 1, head, local_heads)
        key_rows = key_t.T
        value_rows = rows_of(x_ref, 2, head, local_heads).T
        at = slice(head * HEAD_DIM, (head + 1) * HEAD_DIM)
        key_sum[...] = jnp.zeros_like(key_sum)
        value_sum[...] = jnp.zeros_like(value_sum)
        biases = {}
        for block in range(blocks):
            first = window_start(block, blocks, block_frames, window_frames)
            shift = first - block * block_frames
            if shift not in biases:
                biases[shift] = keep_bias(shift, window, block_tokens, count)
            here = slice(block * block_tokens, (block + 1) * block_tokens)
            near = slice(first * FRAME, first * FRAME + window)
            query_here = query_t[:, here]
            up_here = up_ref[at, here]
            scores = dot(key_rows[near], query_here, NN) * (SCORE_SCALE * LOG2_E) + biases[shift]
            weights = jnp.exp2(scores - log_ref[head, :, here])
            inner = jnp.sum(
                up_here.astype(F32) * attended_ref[block, at, :].astype(F32), axis=0, keepdims=True
            )
            prob_grad = dot(value_rows[near], up_here, NN)
            score_grad = (weights * (prob_grad - inner)).astype(BF16)
            rounded = weights.astype(BF16)
            out_ref[block, at, :] = (dot(key_t[:, near], score_grad, NN) * SCORE_SCALE).astype(BF16)
            key_sum[near, :] += dot(score_grad, query_here, NT)
            value_sum[near, :] += dot(rounded, up_here, NT)
        key_grad = (key_sum[...] * SCORE_SCALE).T.astype(BF16)
        value_grad = value_sum[...].T.astype(BF16)
        for block in range(blocks):
            here = slice(block * block_tokens, (block + 1) * block_tokens)
            for part, grad in ((1, key_grad), (2, value_grad)):
                row = (part * local_heads + head) * HEAD_DIM
                out_ref[block, row : row + HEAD_DIM, :] = grad[:, here]


def joined(ref):
    return jnp.concatenate([ref[block] for block in range(ref.shape[0])], axis=1)


def weight_kernel(attended_ref, grad_ref, out_ref, *, column_parts):
    term = dot(joined(attended_ref), grad_ref[...], NN).T
    dp_size = out_ref.shape[0]
    wide = out_ref.shape[1] // column_parts
    for peer in range(dp_size):
        out_ref[peer] = jnp.concatenate(
            [
                term[(part * dp_size + peer) * wide : (part * dp_size + peer + 1) * wide]
                for part in range(column_parts)
            ],
            axis=0,
        ).astype(BF16)


def upstream_kernel(weight_ref, grad_ref, out_ref):
    out_ref[...] = dot(weight_ref[...], grad_ref[...], NT).astype(BF16)


def layer_kernel(attended_ref, weight_ref, out_ref):
    peers, width, tokens = attended_ref.shape
    rows = attended_ref[...].reshape(peers * width, tokens).T
    out_ref[...] = dot(rows, weight_ref[...], NN).astype(BF16)


def per_device(query_in, key_in, value_in, out_grad, out_weight, key_tiles, key_count):
    seq_size = lax.axis_size("seq")
    fsdp_size = lax.axis_size("fh") * lax.axis_size("fl")
    dp_size = lax.axis_size("dp")
    _, local_tokens, model = query_in.shape
    all_tokens = local_tokens * seq_size
    width = model // seq_size
    local_heads = width // HEAD_DIM
    counts = key_count[0]
    smem = pl.BlockSpec(memory_space=pltpu.SMEM)
    vmem = pl.BlockSpec(memory_space=pltpu.VMEM)
    shape = jax.ShapeDtypeStruct

    grad_all = lax.all_gather(out_grad[0], "seq", axis=0, tiled=True)
    packed = call(
        pack_kernel,
        shape((seq_size, 3 * width, local_tokens), BF16),
        (query_in[0], key_in[0], value_in[0]),
    )
    heads = lax.all_to_all(packed, "seq", split_axis=0, concat_axis=0, tiled=True)
    near_weight = lax.all_gather(out_weight, "fl", axis=0, tiled=False)
    row_weight = lax.all_gather(near_weight, "fh", axis=0, tiled=True)
    row_weight = call(join_columns_kernel, shape((width, model), BF16), (row_weight,))
    full_weight = lax.all_gather(row_weight, "seq", axis=0, tiled=True)

    attended, log_total = call(
        forward_kernel,
        (
            shape((seq_size, width, local_tokens), BF16),
            shape((local_heads, 1, all_tokens), F32),
        ),
        (counts, heads),
        in_specs=[smem, vmem],
    )
    attended_tokens = lax.all_to_all(attended, "seq", split_axis=0, concat_axis=0, tiled=True)

    columns = model // (fsdp_size * dp_size)
    term = call(
        functools.partial(weight_kernel, column_parts=fsdp_size),
        shape((dp_size, fsdp_size * columns, width), BF16),
        (attended, grad_all),
    )
    term = lax.all_to_all(term, "dp", split_axis=0, concat_axis=0, tiled=True)
    term = jnp.sum(term.astype(F32), axis=0).astype(BF16)
    term = term.reshape(fsdp_size, columns, width)
    term = lax.all_to_all(term, ("fh", "fl"), split_axis=0, concat_axis=0, tiled=True)
    weight_grad = jnp.sum(term.astype(F32), axis=0).T / (fsdp_size * dp_size)

    upstream = call(upstream_kernel, shape((width, all_tokens), BF16), (row_weight, grad_all))
    grads = call(
        backward_kernel,
        shape((seq_size, 3 * width, local_tokens), BF16),
        (counts, heads, attended, log_total, upstream),
        in_specs=[smem] + [vmem] * 4,
        scratch=[pltpu.VMEM((all_tokens, HEAD_DIM), F32)] * 2,
    )
    grads = lax.all_to_all(grads, "seq", split_axis=0, concat_axis=0, tiled=True)
    query_grad, key_grad, value_grad = call(
        unpack_kernel, (shape((local_tokens, model), BF16),) * 3, (grads,)
    )
    layer_out = call(
        layer_kernel, shape((local_tokens, model), BF16), (attended_tokens, full_weight)
    )
    return (layer_out[None], query_grad[None], key_grad[None], value_grad[None], weight_grad)


def solution(mesh):
    seq_size, fsdp_size, dp_size = (mesh.shape[name] for name in ("seq", "fsdp", "dp"))
    order = [mesh.axis_names.index(name) for name in ("seq", "fsdp", "dp")]
    devices = mesh.devices.transpose(order).reshape(seq_size, fsdp_size // 4, 4, dp_size)
    split_mesh = Mesh(devices, ("seq", "fh", "fl", "dp"))
    clips = ("fh", "fl", "dp")
    tokens = P(clips, "seq", None)
    return jax.shard_map(
        per_device,
        mesh=split_mesh,
        in_specs=(
            tokens,
            tokens,
            tokens,
            tokens,
            P("seq", ("fh", "fl")),
            P(clips, "seq", None, None),
            P(clips, "seq", None),
        ),
        out_specs=(tokens, tokens, tokens, tokens, P("seq", clips)),
        check_vma=False,
    )
```

```python
import functools

import jax
import jax.numpy as jnp
from jax import lax
from jax.experimental import pallas as pl
from jax.experimental.pallas import tpu as pltpu
from jax.sharding import PartitionSpec as P

BF16 = jnp.bfloat16
F32 = jnp.float32
HEAD_DIM = 64
PAIR = 2 * HEAD_DIM
TILE = 32
FRAME = 64
FRAMES = 16
SCORE_SCALE = HEAD_DIM ** (-0.5)
LOG2_E = 1.4426950408889634
DROPPED = -1e30
NT = (((1,), (1,)), ((), ()))
NN = (((1,), (0,)), ((), ()))


def dot(left, right, dims):
    return lax.dot_general(left, right, dims, preferred_element_type=F32)


def call(kernel, out_shape, operands, scalars=0, us=2, after=()):
    vmem = pl.BlockSpec(memory_space=pltpu.VMEM)
    smem = pl.BlockSpec(memory_space=pltpu.SMEM)
    late = len(after)

    def body(*refs):
        kernel(*refs[late:])

    return pl.pallas_call(
        body,
        out_shape=out_shape,
        in_specs=[pl.BlockSpec(memory_space=pl.ANY)] * late
        + [smem] * scalars
        + [vmem] * (len(operands) - scalars),
        out_specs=jax.tree.map(lambda _: vmem, out_shape),
        cost_estimate=pl.CostEstimate(
            flops=int(us * 1e9), bytes_accessed=int(us * 3e6), transcendentals=0
        ),
        compiler_params=pltpu.CompilerParams(vmem_limit_bytes=56 * 2**20),
    )(*after, *operands)


def spread_weight_kernel(weight_ref, count_ref, out_ref, count_out_ref):
    rows, width = weight_ref.shape
    high = rows * width // 128
    piece = 128 - width
    pieces = [weight_ref[high:, at : at + piece] for at in range(0, width, piece)]
    dense = jnp.concatenate([weight_ref[:high, :], jnp.concatenate(pieces, axis=0)], axis=1)
    for peer in range(out_ref.shape[0]):
        out_ref[peer] = dense
    count_out_ref[...] = count_ref[...]


def join_weight_kernel(x_ref, out_ref):
    peers, high, _ = x_ref.shape
    width = out_ref.shape[1] // peers
    piece = 128 - width
    low = out_ref.shape[0] - high
    for peer in range(peers):
        out_ref[:high, peer * width : (peer + 1) * width] = x_ref[peer, :, :width]
        for at in range(width // piece):
            lane = peer * width + at * piece
            out_ref[high:, lane : lane + piece] = x_ref[peer, at * low : (at + 1) * low, width:]


def distances(place, keys, queries):
    key_at = lax.broadcasted_iota(jnp.int32, (keys, 2 * queries), 0)
    query_at = lax.broadcasted_iota(jnp.int32, (keys, 2 * queries), 1) % queries
    key_frame = key_at // FRAME - 1
    frames_off = jnp.abs(key_frame - query_at // FRAME)
    real_frame = key_frame + place * (queries // FRAME)
    frames_off = jnp.where((real_frame >= 0) & (real_frame < FRAMES), frames_off, FRAMES)
    rows_off = jnp.abs((key_at // TILE) % 2 - (query_at // TILE) % 2)
    return frames_off, rows_off


def by_head(first, second, queries):
    at = lax.broadcasted_iota(jnp.int32, (1, 2 * queries), 1)
    return jnp.where(at < queries, first, second)


def masked(scores, gaps, count_ref, pair, queries):
    counts = [count_ref[2 * pair + head, 2] for head in range(2)]
    frame_reach = by_head(*[jnp.where(count >= 3, 1, 0) for count in counts], queries)
    row_reach = by_head(*[jnp.where(count % 2 == 0, 1, 0) for count in counts], queries)
    kept = (gaps[0] <= frame_reach) & (gaps[1] <= row_reach)
    return jnp.where(kept, scores * (SCORE_SCALE * LOG2_E), DROPPED)


def window(left_ref, own_ref, right_ref, part, lanes):
    return jnp.concatenate(
        [left_ref[part, :, lanes], own_ref[:, lanes], right_ref[part, :, lanes]], axis=0
    )


def spread(pair, axis):
    at = lax.broadcasted_iota(jnp.int32, pair.shape, 1 - axis)
    zero = jnp.zeros_like(pair)
    return jnp.concatenate(
        [jnp.where(at < HEAD_DIM, pair, zero), jnp.where(at < HEAD_DIM, zero, pair)], axis=axis
    )


def own_parts(x):
    queries = x.shape[1] // 2
    return jnp.concatenate([x[:HEAD_DIM, :queries], x[HEAD_DIM:, queries:]], axis=0)


def forward_kernel(
    count_ref, place_ref, query_ref, key_ref, value_ref, left_ref, right_ref, attended_ref, log_ref
):
    queries, model = query_ref.shape
    gaps = distances(place_ref[0], queries + 2 * FRAME, queries)
    for pair in range(model // PAIR):
        lanes = slice(pair * PAIR, (pair + 1) * PAIR)
        keys = window(left_ref, key_ref, right_ref, 0, lanes)
        values = window(left_ref, value_ref, right_ref, 1, lanes)
        scores = dot(keys, spread(query_ref[:, lanes], 0), NT)
        scores = masked(scores, gaps, count_ref, pair, queries)
        top = jnp.max(scores, axis=0, keepdims=True)
        raw = jnp.exp2(scores - top)
        total = jnp.sum(raw, axis=0, keepdims=True)
        rounded = (raw * (1.0 / total)).astype(BF16)
        attended_ref[lanes, :] = own_parts(dot(values.T, rounded, NN)).astype(BF16)
        log_ref[pair] = top + jnp.log2(total)


def backward_kernel(
    count_ref, place_ref, query_ref, key_ref, value_ref, left_ref, right_ref, attended_ref, log_ref,
    mixed_ref, query_grad_ref, key_own_ref, value_own_ref, to_left_ref, to_right_ref,
):
    queries, model = query_ref.shape
    gaps = distances(place_ref[0], queries + 2 * FRAME, queries)
    for pair in range(model // PAIR):
        lanes = slice(pair * PAIR, (pair + 1) * PAIR)
        keys = window(left_ref, key_ref, right_ref, 0, lanes)
        values = window(left_ref, value_ref, right_ref, 1, lanes)
        query = spread(query_ref[:, lanes], 0)
        up_t = up_rows(mixed_ref, pair)
        up = spread(up_t, 1)
        scores = masked(dot(keys, query, NT), gaps, count_ref, pair, queries)
        weights = jnp.exp2(scores - log_ref[pair])
        product = up_t.astype(F32) * attended_ref[lanes, :].astype(F32)
        inner = jnp.concatenate(
            [
                jnp.sum(product[:HEAD_DIM], axis=0, keepdims=True),
                jnp.sum(product[HEAD_DIM:], axis=0, keepdims=True),
            ],
            axis=1,
        )
        prob_grad = dot(values, up, NN)
        score_grad = (weights * (prob_grad - inner)).astype(BF16)
        query_grad = own_parts(dot(keys.T, score_grad, NN)) * SCORE_SCALE
        query_grad_ref[:, lanes] = query_grad.T.astype(BF16)
        key_grad = dot(score_grad, query, NN) * SCORE_SCALE
        value_grad = dot(weights.astype(BF16), up, NT)
        for part, (grad, own_ref) in enumerate(
            ((key_grad, key_own_ref), (value_grad, value_own_ref))
        ):
            to_left_ref[part, :, lanes] = grad[:FRAME].astype(BF16)
            own_ref[:, lanes] = grad[FRAME : FRAME + queries]
            to_right_ref[part, :, lanes] = grad[FRAME + queries :].astype(BF16)


def finish_kernel(key_own_ref, value_own_ref, left_ref, right_ref, key_ref, value_ref):
    for part, (own_ref, out_ref) in enumerate(((key_own_ref, key_ref), (value_own_ref, value_ref))):
        out_ref[:FRAME, :] = (own_ref[:FRAME, :] + left_ref[part].astype(F32)).astype(BF16)
        out_ref[FRAME:, :] = (own_ref[FRAME:, :] + right_ref[part].astype(F32)).astype(BF16)


def up_rows(ref, pair):
    width = ref.shape[1] // 2
    pieces = []
    at = pair * PAIR
    while at < (pair + 1) * PAIR:
        end = min((pair + 1) * PAIR, (at // width + 1) * width)
        first = width + at % width
        pieces.append(ref[at // width, first : first + end - at, :])
        at = end
    return pieces[0] if len(pieces) == 1 else jnp.concatenate(pieces, axis=0)


def weight_kernel(mixed_ref, grad_ref, out_ref, *, column_parts):
    peers, rows, _ = mixed_ref.shape
    attended = jnp.concatenate([mixed_ref[peer, : rows // 2, :] for peer in range(peers)], axis=1)
    term = dot(attended, grad_ref[...], NN).T
    dp_size = out_ref.shape[0]
    wide = term.shape[0] // (dp_size * column_parts)
    high = wide * column_parts
    for peer in range(dp_size):
        block = jnp.concatenate(
            [
                term[(part * dp_size + peer) * wide : (part * dp_size + peer + 1) * wide]
                for part in range(column_parts)
            ],
            axis=0,
        )
        out_ref[peer, :high, :] = block[:, :128].astype(BF16)
        out_ref[peer, high:, :] = jnp.concatenate(
            [block[: high // 2, 128:], block[high // 2 :, 128:]], axis=1
        ).astype(BF16)


def sum_kernel(x_ref, out_ref):
    column_parts = out_ref.shape[0]
    high = x_ref.shape[1] * 2 // 3
    wide = high // column_parts
    total = x_ref[0].astype(F32)
    for peer in range(1, x_ref.shape[0]):
        total = total + x_ref[peer].astype(F32)
    rest = jnp.concatenate([total[high:, :64], total[high:, 64:]], axis=0)
    for part in range(column_parts):
        at = part * wide
        first = jnp.concatenate([rest[at : at + 8], rest[at + 8 : at + 16]], axis=1)
        last = jnp.concatenate([rest[at + 16 : at + 24], jnp.zeros((8, 64), F32)], axis=1)
        out_ref[part] = jnp.concatenate([total[at : at + wide], first, last], axis=0).astype(BF16)


def mean_kernel(x_ref, out_ref, *, clips):
    total = x_ref[0].astype(F32)
    for part in range(1, x_ref.shape[0]):
        total = total + x_ref[part].astype(F32)
    rest = jnp.concatenate([total[24:32, :64], total[24:32, 64:], total[32:, :64]], axis=0)
    total = jnp.concatenate([total[:24], rest], axis=1)
    out_ref[...] = total * (1.0 / clips)


def upstream_kernel(weight_ref, grad_ref, attended_ref, out_ref):
    up = dot(weight_ref[...], grad_ref[...], NT).astype(BF16)
    peers, both, tokens = out_ref.shape
    width = both // 2
    for peer in range(peers):
        out_ref[peer, :width, :] = attended_ref[peer * width : (peer + 1) * width, :]
        out_ref[peer, width:, :] = up[:, peer * tokens : (peer + 1) * tokens]


def layer_kernel(attended_ref, weight_ref, out_ref):
    out_ref[...] = dot(attended_ref[...].T, weight_ref[...], NN).astype(BF16)


def per_device(query_in, key_in, value_in, out_grad, out_weight, key_tiles, key_count):
    seq_size = lax.axis_size("seq")
    fsdp_size = lax.axis_size("fsdp")
    dp_size = lax.axis_size("dp")
    query, key, value, grad = query_in[0], key_in[0], value_in[0], out_grad[0]
    tokens, model = query.shape
    width = model // seq_size
    heads = model // HEAD_DIM
    columns = model // (fsdp_size * dp_size)
    shape = jax.ShapeDtypeStruct
    place = lax.axis_index("seq").astype(jnp.int32).reshape(1)
    upward = [(i, i + 1) for i in range(seq_size - 1)]
    downward = [(i + 1, i) for i in range(seq_size - 1)]

    grad_all = lax.all_gather(grad, "seq", axis=0, tiled=True)
    left = lax.ppermute(jnp.stack([key[FRAME:], value[FRAME:]]), "seq", upward)
    right = lax.ppermute(jnp.stack([key[:FRAME], value[:FRAME]]), "seq", downward)
    weight_copies, own_count = call(
        spread_weight_kernel,
        (
            shape((fsdp_size, width * out_weight.shape[1] // 128, 128), BF16),
            shape(key_count.shape[1:], key_count.dtype),
        ),
        (out_weight, key_count[0]),
    )
    weight_copies = lax.all_to_all(weight_copies, "fsdp", split_axis=0, concat_axis=0, tiled=True)
    counts = lax.all_gather(own_count, "seq", axis=0, tiled=True)
    attended, log_total = call(
        forward_kernel,
        (
            shape((model, tokens), BF16),
            shape((heads // 2, 1, 2 * tokens), F32),
        ),
        (counts, place, query, key, value, left, right),
        scalars=2,
        us=7,
    )
    row_weight = call(
        join_weight_kernel, shape((width, model), BF16), (weight_copies,), after=(log_total,)
    )
    full_weight = lax.all_gather(row_weight, "seq", axis=0, tiled=True)
    mixed = call(
        upstream_kernel,
        shape((seq_size, 2 * width, tokens), BF16),
        (row_weight, grad_all, attended),
        us=4,
    )
    mixed = lax.all_to_all(mixed, "seq", split_axis=0, concat_axis=0, tiled=True)

    term = call(
        functools.partial(weight_kernel, column_parts=fsdp_size),
        shape((dp_size, fsdp_size * columns * width // 128, 128), BF16),
        (mixed, grad_all),
        us=4,
    )
    query_grad, key_own, value_own, to_left, to_right = call(
        backward_kernel,
        (
            shape((tokens, model), BF16),
            shape((tokens, model), F32),
            shape((tokens, model), F32),
            shape((2, FRAME, model), BF16),
            shape((2, FRAME, model), BF16),
        ),
        (counts, place, query, key, value, left, right, attended, log_total, mixed),
        scalars=2,
        us=7,
    )
    term = lax.all_to_all(term, "dp", split_axis=0, concat_axis=0, tiled=True)
    term = call(sum_kernel, shape((fsdp_size, columns + 16, 128), BF16), (term,), after=(to_left,))
    term = lax.all_to_all(term, "fsdp", split_axis=0, concat_axis=0, tiled=True)
    from_left = lax.ppermute(to_right, "seq", upward)
    from_right = lax.ppermute(to_left, "seq", downward)
    key_grad, value_grad = call(
        finish_kernel, (shape((tokens, model), BF16),) * 2, (key_own, value_own, from_left, from_right)
    )
    layer_out = call(layer_kernel, shape((tokens, model), BF16), (attended, full_weight), us=4)
    weight_grad = call(
        functools.partial(mean_kernel, clips=fsdp_size * dp_size),
        shape((columns, width), F32),
        (term,),
        after=(key_grad, layer_out),
    ).T

    return (layer_out[None], query_grad[None], key_grad[None], value_grad[None], weight_grad)


def solution(mesh):
    clips = ("fsdp", "dp")
    tokens = P(clips, "seq", None)
    return jax.shard_map(
        per_device,
        mesh=mesh,
        in_specs=(
            tokens,
            tokens,
            tokens,
            tokens,
            P("seq", "fsdp"),
            P(clips, "seq", None, None),
            P(clips, "seq", None),
        ),
        out_specs=(tokens, tokens, tokens, tokens, P("seq", clips)),
        check_vma=False,
    )
```

```python
import functools

import jax
import jax.numpy as jnp
from jax import lax
from jax.experimental import pallas as pl
from jax.experimental.pallas import tpu as pltpu
from jax.sharding import PartitionSpec as P

BF16 = jnp.bfloat16
F32 = jnp.float32
HEAD_DIM = 64
PAIR = 2 * HEAD_DIM
TILE = 32
FRAME = 64
FRAMES = 16
SCORE_SCALE = HEAD_DIM ** (-0.5)
LOG2_E = 1.4426950408889634
DROPPED = -1e30
NT = (((1,), (1,)), ((), ()))
NN = (((1,), (0,)), ((), ()))


def dot(left, right, dims):
    return lax.dot_general(left, right, dims, preferred_element_type=F32)


def call(kernel, out_shape, operands, scalars=0, us=2, after=()):
    vmem = pl.BlockSpec(memory_space=pltpu.VMEM)
    smem = pl.BlockSpec(memory_space=pltpu.SMEM)
    late = len(after)

    def body(*refs):
        kernel(*refs[late:])

    return pl.pallas_call(
        body,
        out_shape=out_shape,
        in_specs=[pl.BlockSpec(memory_space=pl.ANY)] * late
        + [smem] * scalars
        + [vmem] * (len(operands) - scalars),
        out_specs=jax.tree.map(lambda _: vmem, out_shape),
        cost_estimate=pl.CostEstimate(
            flops=int(us * 1e9), bytes_accessed=int(us * 3e6), transcendentals=0
        ),
        compiler_params=pltpu.CompilerParams(vmem_limit_bytes=56 * 2**20),
    )(*after, *operands)


def held_until(x, after):
    anywhere = pl.BlockSpec(memory_space=pl.ANY)

    def body(*refs):
        pass

    return pl.pallas_call(
        body,
        out_shape=jax.ShapeDtypeStruct(x.shape, x.dtype),
        in_specs=[anywhere] * (1 + len(after)),
        out_specs=anywhere,
        input_output_aliases={0: 0},
    )(x, *after)


def spread_weight_kernel(weight_ref, out_ref):
    rows, width = weight_ref.shape
    high = rows * width // 128
    piece = 128 - width
    pieces = [weight_ref[high:, at : at + piece] for at in range(0, width, piece)]
    dense = jnp.concatenate([weight_ref[:high, :], jnp.concatenate(pieces, axis=0)], axis=1)
    for peer in range(out_ref.shape[0]):
        out_ref[peer] = dense


def join_weight_kernel(x_ref, out_ref):
    peers, high, _ = x_ref.shape
    width = out_ref.shape[1] // peers
    piece = 128 - width
    low = out_ref.shape[0] - high
    for peer in range(peers):
        out_ref[:high, peer * width : (peer + 1) * width] = x_ref[peer, :, :width]
        for at in range(width // piece):
            lane = peer * width + at * piece
            out_ref[high:, lane : lane + piece] = x_ref[peer, at * low : (at + 1) * low, width:]


def distances(place, keys, queries):
    key_at = lax.broadcasted_iota(jnp.int32, (keys, 2 * queries), 0)
    query_at = lax.broadcasted_iota(jnp.int32, (keys, 2 * queries), 1) % queries
    key_frame = key_at // FRAME - 1
    frames_off = jnp.abs(key_frame - query_at // FRAME)
    real_frame = key_frame + place * (queries // FRAME)
    frames_off = jnp.where((real_frame >= 0) & (real_frame < FRAMES), frames_off, FRAMES)
    rows_off = jnp.abs((key_at // TILE) % 2 - (query_at // TILE) % 2)
    return frames_off, rows_off


def by_head(first, second, queries):
    at = lax.broadcasted_iota(jnp.int32, (1, 2 * queries), 1)
    return jnp.where(at < queries, first, second)


def masked(scores, gaps, count_ref, pair, queries):
    counts = [count_ref[2 * pair + head, 2] for head in range(2)]
    frame_reach = by_head(*[jnp.where(count >= 3, 1, 0) for count in counts], queries)
    row_reach = by_head(*[jnp.where(count % 2 == 0, 1, 0) for count in counts], queries)
    kept = (gaps[0] <= frame_reach) & (gaps[1] <= row_reach)
    return jnp.where(kept, scores * (SCORE_SCALE * LOG2_E), DROPPED)


def window(left_ref, own_ref, right_ref, part, lanes):
    return jnp.concatenate(
        [left_ref[part, :, lanes], own_ref[:, lanes], right_ref[part, :, lanes]], axis=0
    )


def spread(pair, axis):
    at = lax.broadcasted_iota(jnp.int32, pair.shape, 1 - axis)
    zero = jnp.zeros_like(pair)
    return jnp.concatenate(
        [jnp.where(at < HEAD_DIM, pair, zero), jnp.where(at < HEAD_DIM, zero, pair)], axis=axis
    )


def own_parts(x):
    queries = x.shape[1] // 2
    return jnp.concatenate([x[:HEAD_DIM, :queries], x[HEAD_DIM:, queries:]], axis=0)


def forward_kernel(
    count_ref, place_ref, query_ref, key_ref, value_ref, left_ref, right_ref, attended_ref, log_ref
):
    queries, model = query_ref.shape
    gaps = distances(place_ref[0], queries + 2 * FRAME, queries)
    for pair in range(model // PAIR):
        lanes = slice(pair * PAIR, (pair + 1) * PAIR)
        keys = window(left_ref, key_ref, right_ref, 0, lanes)
        values = window(left_ref, value_ref, right_ref, 1, lanes)
        scores = dot(keys, spread(query_ref[:, lanes], 0), NT)
        scores = masked(scores, gaps, count_ref, pair, queries)
        top = jnp.max(scores, axis=0, keepdims=True)
        raw = jnp.exp2(scores - top)
        total = jnp.sum(raw, axis=0, keepdims=True)
        rounded = (raw * (1.0 / total)).astype(BF16)
        attended_ref[lanes, :] = own_parts(dot(values.T, rounded, NN)).astype(BF16)
        log_ref[pair] = top + jnp.log2(total)


def backward_kernel(
    count_ref, place_ref, query_ref, key_ref, value_ref, left_ref, right_ref, attended_ref, log_ref,
    mixed_ref, query_grad_ref, key_own_ref, value_own_ref, to_left_ref, to_right_ref,
):
    queries, model = query_ref.shape
    gaps = distances(place_ref[0], queries + 2 * FRAME, queries)
    for pair in range(model // PAIR):
        lanes = slice(pair * PAIR, (pair + 1) * PAIR)
        keys = window(left_ref, key_ref, right_ref, 0, lanes)
        values = window(left_ref, value_ref, right_ref, 1, lanes)
        query = spread(query_ref[:, lanes], 0)
        up_t = up_rows(mixed_ref, pair)
        up = spread(up_t, 1)
        scores = masked(dot(keys, query, NT), gaps, count_ref, pair, queries)
        weights = jnp.exp2(scores - log_ref[pair])
        product = up_t.astype(F32) * attended_ref[lanes, :].astype(F32)
        inner = jnp.concatenate(
            [
                jnp.sum(product[:HEAD_DIM], axis=0, keepdims=True),
                jnp.sum(product[HEAD_DIM:], axis=0, keepdims=True),
            ],
            axis=1,
        )
        prob_grad = dot(values, up, NN)
        score_grad = (weights * (prob_grad - inner)).astype(BF16)
        query_grad = own_parts(dot(keys.T, score_grad, NN)) * SCORE_SCALE
        query_grad_ref[:, lanes] = query_grad.T.astype(BF16)
        key_grad = dot(score_grad, query, NN) * SCORE_SCALE
        value_grad = dot(weights.astype(BF16), up, NT)
        for part, (grad, own_ref) in enumerate(
            ((key_grad, key_own_ref), (value_grad, value_own_ref))
        ):
            to_left_ref[part, :, lanes] = grad[:FRAME].astype(BF16)
            own_ref[:, lanes] = grad[FRAME : FRAME + queries]
            to_right_ref[part, :, lanes] = grad[FRAME + queries :].astype(BF16)


def finish_kernel(key_own_ref, value_own_ref, left_ref, right_ref, key_ref, value_ref):
    for part, (own_ref, out_ref) in enumerate(((key_own_ref, key_ref), (value_own_ref, value_ref))):
        out_ref[:FRAME, :] = (own_ref[:FRAME, :] + left_ref[part].astype(F32)).astype(BF16)
        out_ref[FRAME:, :] = (own_ref[FRAME:, :] + right_ref[part].astype(F32)).astype(BF16)


def up_rows(ref, pair):
    width = ref.shape[1] // 2
    pieces = []
    at = pair * PAIR
    while at < (pair + 1) * PAIR:
        end = min((pair + 1) * PAIR, (at // width + 1) * width)
        first = width + at % width
        pieces.append(ref[at // width, first : first + end - at, :])
        at = end
    return pieces[0] if len(pieces) == 1 else jnp.concatenate(pieces, axis=0)


def weight_kernel(mixed_ref, grad_ref, out_ref, *, column_parts):
    peers, rows, _ = mixed_ref.shape
    attended = jnp.concatenate([mixed_ref[peer, : rows // 2, :] for peer in range(peers)], axis=1)
    term = dot(attended, grad_ref[...], NN).T
    dp_size = out_ref.shape[0]
    wide = term.shape[0] // (dp_size * column_parts)
    high = wide * column_parts
    for peer in range(dp_size):
        block = jnp.concatenate(
            [
                term[(part * dp_size + peer) * wide : (part * dp_size + peer + 1) * wide]
                for part in range(column_parts)
            ],
            axis=0,
        )
        out_ref[peer, :high, :] = block[:, :128].astype(BF16)
        out_ref[peer, high:, :] = jnp.concatenate(
            [block[: high // 2, 128:], block[high // 2 :, 128:]], axis=1
        ).astype(BF16)


def sum_kernel(x_ref, out_ref):
    column_parts = out_ref.shape[0]
    high = x_ref.shape[1] * 2 // 3
    wide = high // column_parts
    total = x_ref[0].astype(F32)
    for peer in range(1, x_ref.shape[0]):
        total = total + x_ref[peer].astype(F32)
    rest = jnp.concatenate([total[high:, :64], total[high:, 64:]], axis=0)
    for part in range(column_parts):
        at = part * wide
        first = jnp.concatenate([rest[at : at + 8], rest[at + 8 : at + 16]], axis=1)
        last = jnp.concatenate([rest[at + 16 : at + 24], jnp.zeros((8, 64), F32)], axis=1)
        out_ref[part] = jnp.concatenate([total[at : at + wide], first, last], axis=0).astype(BF16)


def mean_kernel(x_ref, out_ref, *, clips):
    total = x_ref[0].astype(F32)
    for part in range(1, x_ref.shape[0]):
        total = total + x_ref[part].astype(F32)
    rest = jnp.concatenate([total[24:32, :64], total[24:32, 64:], total[32:, :64]], axis=0)
    total = jnp.concatenate([total[:24], rest], axis=1)
    out_ref[...] = total * (1.0 / clips)


def upstream_kernel(weight_ref, grad_ref, attended_ref, out_ref):
    up = dot(grad_ref[...], weight_ref[...], NT).T.astype(BF16)
    peers, both, tokens = out_ref.shape
    width = both // 2
    for peer in range(peers):
        out_ref[peer, :width, :] = attended_ref[peer * width : (peer + 1) * width, :]
        out_ref[peer, width:, :] = up[:, peer * tokens : (peer + 1) * tokens]


def layer_kernel(attended_ref, weight_ref, out_ref):
    out_ref[...] = dot(attended_ref[...].T, weight_ref[...], NN).astype(BF16)


def per_device(query_in, key_in, value_in, out_grad, out_weight, key_tiles, key_count):
    seq_size = lax.axis_size("seq")
    fsdp_size = lax.axis_size("fsdp")
    dp_size = lax.axis_size("dp")
    query, key, value, grad = query_in[0], key_in[0], value_in[0], out_grad[0]
    tokens, model = query.shape
    width = model // seq_size
    heads = model // HEAD_DIM
    columns = model // (fsdp_size * dp_size)
    shape = jax.ShapeDtypeStruct
    place = lax.axis_index("seq").astype(jnp.int32).reshape(1)
    upward = [(i, i + 1) for i in range(seq_size - 1)]
    downward = [(i + 1, i) for i in range(seq_size - 1)]

    grad_all = lax.all_gather(grad, "seq", axis=0, tiled=True)
    left = lax.ppermute(jnp.stack([key[FRAME:], value[FRAME:]]), "seq", upward)
    right = lax.ppermute(jnp.stack([key[:FRAME], value[:FRAME]]), "seq", downward)
    weight_copies = call(
        spread_weight_kernel,
        shape((fsdp_size, width * out_weight.shape[1] // 128, 128), BF16),
        (out_weight,),
    )
    own_count = held_until(key_count[0], (weight_copies,))
    weight_copies = lax.all_to_all(weight_copies, "fsdp", split_axis=0, concat_axis=0, tiled=True)
    counts = lax.all_gather(own_count, "seq", axis=0, tiled=True)

    attended, log_total = call(
        forward_kernel,
        (
            shape((model, tokens), BF16),
            shape((heads // 2, 1, 2 * tokens), F32),
        ),
        (counts, place, query, key, value, left, right),
        scalars=2,
        us=7,
    )
    row_weight = call(
        join_weight_kernel, shape((width, model), BF16), (weight_copies,), after=(log_total,)
    )
    full_weight = lax.all_gather(row_weight, "seq", axis=0, tiled=True)
    mixed = call(
        upstream_kernel,
        shape((seq_size, 2 * width, tokens), BF16),
        (row_weight, grad_all, attended),
        us=4,
    )
    mixed = lax.all_to_all(mixed, "seq", split_axis=0, concat_axis=0, tiled=True)

    term = call(
        functools.partial(weight_kernel, column_parts=fsdp_size),
        shape((dp_size, fsdp_size * columns * width // 128, 128), BF16),
        (mixed, grad_all),
        us=4,
    )
    query_grad, key_own, value_own, to_left, to_right = call(
        backward_kernel,
        (
            shape((tokens, model), BF16),
            shape((tokens, model), F32),
            shape((tokens, model), F32),
            shape((2, FRAME, model), BF16),
            shape((2, FRAME, model), BF16),
        ),
        (counts, place, query, key, value, left, right, attended, log_total, mixed),
        scalars=2,
        us=7,
    )
    term = lax.all_to_all(term, "dp", split_axis=0, concat_axis=0, tiled=True)
    summed = call(sum_kernel, shape((fsdp_size, columns + 16, 128), BF16), (term,), after=(to_left,))
    term = lax.all_to_all(summed, "fsdp", split_axis=0, concat_axis=0, tiled=True)
    from_left = lax.ppermute(held_until(to_right, (summed,)), "seq", upward)
    from_right = lax.ppermute(held_until(to_left, (summed,)), "seq", downward)
    key_grad, value_grad = call(
        finish_kernel, (shape((tokens, model), BF16),) * 2, (key_own, value_own, from_left, from_right)
    )
    layer_out = call(layer_kernel, shape((tokens, model), BF16), (attended, full_weight), us=4)
    weight_grad = call(
        functools.partial(mean_kernel, clips=fsdp_size * dp_size),
        shape((columns, width), F32),
        (term,),
        after=(key_grad, layer_out),
    ).T

    return (layer_out[None], query_grad[None], key_grad[None], value_grad[None], weight_grad)


def solution(mesh):
    clips = ("fsdp", "dp")
    tokens = P(clips, "seq", None)
    return jax.shard_map(
        per_device,
        mesh=mesh,
        in_specs=(
            tokens,
            tokens,
            tokens,
            tokens,
            P("seq", "fsdp"),
            P(clips, "seq", None, None),
            P(clips, "seq", None),
        ),
        out_specs=(tokens, tokens, tokens, tokens, P("seq", clips)),
        check_vma=False,
    )
```

```python
import functools

import jax
import jax.numpy as jnp
from jax import lax
from jax.experimental import pallas as pl
from jax.experimental.pallas import tpu as pltpu
from jax.sharding import PartitionSpec as P

BF16 = jnp.bfloat16
F32 = jnp.float32
HEAD_DIM = 64
PAIR = 2 * HEAD_DIM
TILE = 32
FRAME = 64
FRAMES = 16
SCORE_SCALE = HEAD_DIM ** (-0.5)
LOG2_E = 1.4426950408889634
DROPPED = -1e30
NT = (((1,), (1,)), ((), ()))
NN = (((1,), (0,)), ((), ()))


def dot(left, right, dims):
    return lax.dot_general(left, right, dims, preferred_element_type=F32)


def call(kernel, out_shape, operands, scalars=0, us=2, after=()):
    vmem = pl.BlockSpec(memory_space=pltpu.VMEM)
    smem = pl.BlockSpec(memory_space=pltpu.SMEM)
    late = len(after)

    def body(*refs):
        kernel(*refs[late:])

    return pl.pallas_call(
        body,
        out_shape=out_shape,
        in_specs=[pl.BlockSpec(memory_space=pl.ANY)] * late
        + [smem] * scalars
        + [vmem] * (len(operands) - scalars),
        out_specs=jax.tree.map(lambda _: vmem, out_shape),
        cost_estimate=pl.CostEstimate(
            flops=int(us * 1e9), bytes_accessed=int(us * 3e6), transcendentals=0
        ),
        compiler_params=pltpu.CompilerParams(vmem_limit_bytes=56 * 2**20),
    )(*after, *operands)


def held_until(x, after):
    anywhere = pl.BlockSpec(memory_space=pl.ANY)

    def body(*refs):
        pass

    return pl.pallas_call(
        body,
        out_shape=jax.ShapeDtypeStruct(x.shape, x.dtype),
        in_specs=[anywhere] * (1 + len(after)),
        out_specs=anywhere,
        input_output_aliases={0: 0},
    )(x, *after)


def spread_weight_kernel(weight_ref, out_ref):
    rows, width = weight_ref.shape
    high = rows * width // 128
    piece = 128 - width
    pieces = [weight_ref[high:, at : at + piece] for at in range(0, width, piece)]
    dense = jnp.concatenate([weight_ref[:high, :], jnp.concatenate(pieces, axis=0)], axis=1)
    for peer in range(out_ref.shape[0]):
        out_ref[peer] = dense


def join_weight_kernel(x_ref, out_ref):
    peers, high, _ = x_ref.shape
    width = out_ref.shape[1] // peers
    piece = 128 - width
    low = out_ref.shape[0] - high
    for peer in range(peers):
        out_ref[:high, peer * width : (peer + 1) * width] = x_ref[peer, :, :width]
        for at in range(width // piece):
            lane = peer * width + at * piece
            out_ref[high:, lane : lane + piece] = x_ref[peer, at * low : (at + 1) * low, width:]


def distances(place, keys, queries):
    key_at = lax.broadcasted_iota(jnp.int32, (keys, 2 * queries), 0)
    query_at = lax.broadcasted_iota(jnp.int32, (keys, 2 * queries), 1) % queries
    key_frame = key_at // FRAME - 1
    frames_off = jnp.abs(key_frame - query_at // FRAME)
    real_frame = key_frame + place * (queries // FRAME)
    frames_off = jnp.where((real_frame >= 0) & (real_frame < FRAMES), frames_off, FRAMES)
    rows_off = jnp.abs((key_at // TILE) % 2 - (query_at // TILE) % 2)
    return frames_off, rows_off


def by_head(first, second, queries):
    at = lax.broadcasted_iota(jnp.int32, (1, 2 * queries), 1)
    return jnp.where(at < queries, first, second)


def masked(scores, gaps, count_ref, pair, queries):
    counts = [count_ref[2 * pair + head, 2] for head in range(2)]
    frame_reach = by_head(*[jnp.where(count >= 3, 1, 0) for count in counts], queries)
    row_reach = by_head(*[jnp.where(count % 2 == 0, 1, 0) for count in counts], queries)
    kept = (gaps[0] <= frame_reach) & (gaps[1] <= row_reach)
    return jnp.where(kept, scores * (SCORE_SCALE * LOG2_E), DROPPED)


def window(left_ref, own_ref, right_ref, part, lanes):
    return jnp.concatenate(
        [left_ref[part, :, lanes], own_ref[:, lanes], right_ref[part, :, lanes]], axis=0
    )


def spread(pair, axis):
    at = lax.broadcasted_iota(jnp.int32, pair.shape, 1 - axis)
    zero = jnp.zeros_like(pair)
    return jnp.concatenate(
        [jnp.where(at < HEAD_DIM, pair, zero), jnp.where(at < HEAD_DIM, zero, pair)], axis=axis
    )


def own_parts(x):
    queries = x.shape[1] // 2
    return jnp.concatenate([x[:HEAD_DIM, :queries], x[HEAD_DIM:, queries:]], axis=0)


def forward_kernel(
    count_ref, place_ref, query_ref, key_ref, value_ref, left_ref, right_ref, attended_ref, log_ref
):
    queries, model = query_ref.shape
    gaps = distances(place_ref[0], queries + 2 * FRAME, queries)
    for pair in range(model // PAIR):
        lanes = slice(pair * PAIR, (pair + 1) * PAIR)
        keys = window(left_ref, key_ref, right_ref, 0, lanes)
        values = window(left_ref, value_ref, right_ref, 1, lanes)
        scores = dot(keys, spread(query_ref[:, lanes], 0), NT)
        scores = masked(scores, gaps, count_ref, pair, queries)
        top = jnp.max(scores, axis=0, keepdims=True)
        raw = jnp.exp2(scores - top)
        total = jnp.sum(raw, axis=0, keepdims=True)
        rounded = (raw * (1.0 / total)).astype(BF16)
        attended_ref[lanes, :] = own_parts(dot(values.T, rounded, NN)).astype(BF16)
        log_ref[pair] = top + jnp.log2(total)


def backward_kernel(
    count_ref, place_ref, query_ref, key_ref, value_ref, left_ref, right_ref, attended_ref, log_ref,
    mixed_ref, query_grad_ref, key_own_ref, value_own_ref, to_left_ref, to_right_ref,
):
    queries, model = query_ref.shape
    gaps = distances(place_ref[0], queries + 2 * FRAME, queries)
    for pair in range(model // PAIR):
        lanes = slice(pair * PAIR, (pair + 1) * PAIR)
        keys = window(left_ref, key_ref, right_ref, 0, lanes)
        values = window(left_ref, value_ref, right_ref, 1, lanes)
        query = spread(query_ref[:, lanes], 0)
        up_t = up_rows(mixed_ref, pair)
        up = spread(up_t, 1)
        scores = masked(dot(keys, query, NT), gaps, count_ref, pair, queries)
        weights = jnp.exp2(scores - log_ref[pair])
        product = up_t.astype(F32) * attended_ref[lanes, :].astype(F32)
        inner = jnp.concatenate(
            [
                jnp.sum(product[:HEAD_DIM], axis=0, keepdims=True),
                jnp.sum(product[HEAD_DIM:], axis=0, keepdims=True),
            ],
            axis=1,
        )
        prob_grad = dot(values, up, NN)
        score_grad = (weights * (prob_grad - inner)).astype(BF16)
        query_grad = own_parts(dot(keys.T, score_grad, NN)) * SCORE_SCALE
        query_grad_ref[:, lanes] = query_grad.T.astype(BF16)
        key_grad = dot(score_grad, query, NN) * SCORE_SCALE
        value_grad = dot(weights.astype(BF16), up, NT)
        for part, (grad, own_ref) in enumerate(
            ((key_grad, key_own_ref), (value_grad, value_own_ref))
        ):
            to_left_ref[part, :, lanes] = grad[:FRAME].astype(BF16)
            own_ref[:, lanes] = grad[FRAME : FRAME + queries]
            to_right_ref[part, :, lanes] = grad[FRAME + queries :].astype(BF16)


def finish_kernel(key_own_ref, value_own_ref, left_ref, right_ref, key_ref, value_ref):
    for part, (own_ref, out_ref) in enumerate(((key_own_ref, key_ref), (value_own_ref, value_ref))):
        out_ref[:FRAME, :] = (own_ref[:FRAME, :] + left_ref[part].astype(F32)).astype(BF16)
        out_ref[FRAME:, :] = (own_ref[FRAME:, :] + right_ref[part].astype(F32)).astype(BF16)


def up_rows(ref, pair):
    width = ref.shape[1] // 2
    pieces = []
    at = pair * PAIR
    while at < (pair + 1) * PAIR:
        end = min((pair + 1) * PAIR, (at // width + 1) * width)
        first = width + at % width
        pieces.append(ref[at // width, first : first + end - at, :])
        at = end
    return pieces[0] if len(pieces) == 1 else jnp.concatenate(pieces, axis=0)


def weight_kernel(mixed_ref, grad_ref, out_ref, *, column_parts):
    peers, rows, _ = mixed_ref.shape
    attended = jnp.concatenate([mixed_ref[peer, : rows // 2, :] for peer in range(peers)], axis=1)
    term = dot(attended, grad_ref[...], NN).T
    dp_size = out_ref.shape[0]
    wide = term.shape[0] // (dp_size * column_parts)
    high = wide * column_parts
    for peer in range(dp_size):
        block = jnp.concatenate(
            [
                term[(part * dp_size + peer) * wide : (part * dp_size + peer + 1) * wide]
                for part in range(column_parts)
            ],
            axis=0,
        )
        out_ref[peer, :high, :] = block[:, :128].astype(BF16)
        out_ref[peer, high:, :] = jnp.concatenate(
            [block[: high // 2, 128:], block[high // 2 :, 128:]], axis=1
        ).astype(BF16)


def sum_kernel(x_ref, out_ref):
    column_parts = out_ref.shape[0]
    high = x_ref.shape[1] * 2 // 3
    wide = high // column_parts
    total = x_ref[0].astype(F32)
    for peer in range(1, x_ref.shape[0]):
        total = total + x_ref[peer].astype(F32)
    rest = jnp.concatenate([total[high:, :64], total[high:, 64:]], axis=0)
    for part in range(column_parts):
        at = part * wide
        first = jnp.concatenate([rest[at : at + 8], rest[at + 8 : at + 16]], axis=1)
        last = jnp.concatenate([rest[at + 16 : at + 24], jnp.zeros((8, 64), F32)], axis=1)
        out_ref[part] = jnp.concatenate([total[at : at + wide], first, last], axis=0).astype(BF16)


def mean_kernel(x_ref, out_ref, *, clips):
    total = x_ref[0].astype(F32)
    for part in range(1, x_ref.shape[0]):
        total = total + x_ref[part].astype(F32)
    rest = jnp.concatenate([total[24:32, :64], total[24:32, 64:], total[32:, :64]], axis=0)
    total = jnp.concatenate([total[:24], rest], axis=1)
    out_ref[...] = total * (1.0 / clips)


def upstream_kernel(weight_ref, grad_ref, attended_ref, out_ref):
    up = dot(grad_ref[...], weight_ref[...], NT).T.astype(BF16)
    peers, both, tokens = out_ref.shape
    width = both // 2
    for peer in range(peers):
        out_ref[peer, :width, :] = attended_ref[peer * width : (peer + 1) * width, :]
        out_ref[peer, width:, :] = up[:, peer * tokens : (peer + 1) * tokens]


def layer_kernel(attended_ref, weight_ref, out_ref):
    out_ref[...] = dot(attended_ref[...].T, weight_ref[...], NN).astype(BF16)


def per_device(query_in, key_in, value_in, out_grad, out_weight, key_tiles, key_count):
    seq_size = lax.axis_size("seq")
    fsdp_size = lax.axis_size("fsdp")
    dp_size = lax.axis_size("dp")
    query, key, value, grad = query_in[0], key_in[0], value_in[0], out_grad[0]
    tokens, model = query.shape
    width = model // seq_size
    heads = model // HEAD_DIM
    columns = model // (fsdp_size * dp_size)
    shape = jax.ShapeDtypeStruct
    place = lax.axis_index("seq").astype(jnp.int32).reshape(1)
    upward = [(i, i + 1) for i in range(seq_size - 1)]
    downward = [(i + 1, i) for i in range(seq_size - 1)]

    grad_all = lax.all_gather(grad, "seq", axis=0, tiled=True)
    left = lax.ppermute(jnp.stack([key[FRAME:], value[FRAME:]]), "seq", upward)
    right = lax.ppermute(jnp.stack([key[:FRAME], value[:FRAME]]), "seq", downward)
    weight_copies = call(
        spread_weight_kernel,
        shape((fsdp_size, width * out_weight.shape[1] // 128, 128), BF16),
        (out_weight,),
    )
    own_count = held_until(key_count[0], (weight_copies,))
    weight_copies = lax.all_to_all(weight_copies, "fsdp", split_axis=0, concat_axis=0, tiled=True)
    counts = lax.all_gather(own_count, "seq", axis=0, tiled=True)

    attended, log_total = call(
        forward_kernel,
        (
            shape((model, tokens), BF16),
            shape((heads // 2, 1, 2 * tokens), F32),
        ),
        (counts, place, query, key, value, left, right),
        scalars=2,
        us=7,
    )
    row_weight = call(
        join_weight_kernel, shape((width, model), BF16), (weight_copies,), after=(log_total,)
    )
    full_weight = lax.all_gather(row_weight, "seq", axis=0, tiled=True)
    mixed = call(
        upstream_kernel,
        shape((seq_size, 2 * width, tokens), BF16),
        (row_weight, grad_all, attended),
        us=4,
    )
    mixed = lax.all_to_all(mixed, "seq", split_axis=0, concat_axis=0, tiled=True)

    term = call(
        functools.partial(weight_kernel, column_parts=fsdp_size),
        shape((dp_size, fsdp_size * columns * width // 128, 128), BF16),
        (mixed, grad_all),
        us=4,
    )
    query_grad, key_own, value_own, to_left, to_right = call(
        backward_kernel,
        (
            shape((tokens, model), BF16),
            shape((tokens, model), F32),
            shape((tokens, model), F32),
            shape((2, FRAME, model), BF16),
            shape((2, FRAME, model), BF16),
        ),
        (counts, place, query, key, value, left, right, attended, log_total, mixed),
        scalars=2,
        us=7,
    )
    term = lax.all_to_all(term, "dp", split_axis=0, concat_axis=0, tiled=True)
    summed = call(sum_kernel, shape((fsdp_size, columns + 16, 128), BF16), (term,), after=(to_left,))
    term = lax.all_to_all(summed, "fsdp", split_axis=0, concat_axis=0, tiled=True)
    layer_out = call(layer_kernel, shape((tokens, model), BF16), (attended, full_weight), us=4, after=(summed,))
    from_left = lax.ppermute(held_until(to_right, (layer_out,)), "seq", upward)
    from_right = lax.ppermute(held_until(to_left, (layer_out,)), "seq", downward)
    key_grad, value_grad = call(
        finish_kernel, (shape((tokens, model), BF16),) * 2, (key_own, value_own, from_left, from_right)
    )
    weight_grad = call(
        functools.partial(mean_kernel, clips=fsdp_size * dp_size),
        shape((columns, width), F32),
        (term,),
        after=(key_grad, layer_out),
    ).T

    return (layer_out[None], query_grad[None], key_grad[None], value_grad[None], weight_grad)


def solution(mesh):
    clips = ("fsdp", "dp")
    tokens = P(clips, "seq", None)
    return jax.shard_map(
        per_device,
        mesh=mesh,
        in_specs=(
            tokens,
            tokens,
            tokens,
            tokens,
            P("seq", "fsdp"),
            P(clips, "seq", None, None),
            P(clips, "seq", None),
        ),
        out_specs=(tokens, tokens, tokens, tokens, P("seq", clips)),
        check_vma=False,
    )
```
